32 devices in a mesh: book: 2 (over y), seq: 4 (over x, core), sub: 4 (over z).
Axes of the slice: x: 2, y: 2, z: 4, core: 2. Of those that a mesh axis runs over, the one named last changes fastest.
Arguments:
- queries: bfloat16 [16384, 2048], P(('book', 'seq'), 'sub'), parts along dimension 0, may hold values from -4 to 1920
- keys: bfloat16 [16384, 2048], P(('book', 'seq'), 'sub'), parts along dimension 0, may hold values from -6 to 4
- values: bfloat16 [16384, 2048], P(('book', 'seq'), 'sub'), parts along dimension 0, may hold values from -6 to 6
- decay: float32 [8, 8], P('book', 'sub'), parts along dimension 0, may hold values from 0.05 to 1
- gate: float32 [8], P('sub'), may hold values from -0.5 to 3
- summary: bfloat16 [512, 2048], P(('book', 'seq')), parts along dimension 0, may hold values from -6 to 6
- wq_sum: bfloat16 [2048, 2048], P(None, 'sub'), may hold values from -0.25 to 0.25
- wo_sum: bfloat16 [2048, 2048], P('sub'), may hold values from -0.125 to 0.125
Outputs:
- attended: bfloat16 [16384, 2048], P(('book', 'seq'), 'sub'), parts along dimension 0
- summarized: bfloat16 [512, 2048], P(('book', 'seq')), parts along dimension 0
The draws below stay inside these ranges and needn't reach their ends.
There are 2 independent parts, one for each index of `book`. The reference program is written for one: setup_inputs(seed, part) draws one part's arguments, and reference() takes and returns one part's arrays. A program takes and returns all parts, laid end to end along the dimension named above; an argument that names none is the same for every part. Nothing has to cross between parts.
All inputs are finite; a program needn't handle non-finite values.
Results may differ from the reference program's by a relative error of at most 0.019.
Values may be sent and summed in bfloat16 or wider, within the bound.
A program may use at most 128 MiB of HBM per device.

```python
import jax
import jax.numpy as jnp
from jax import lax

D = 2048
HEAD_TOTAL = 8
DH = 256
SEG = 2048
STEPS = 4
SEGMENT_TOTAL = 4
TOKENS = 8192
SUMROWS = 256


def query_key_couple(key):
    keys_split = jax.random.split(jax.random.fold_in(key, 11), 4)
    head_shape = (TOKENS, HEAD_TOTAL, DH)
    chosen = jax.random.randint(keys_split[0], (TOKENS, HEAD_TOTAL), 0, DH)
    hot_mask = jnp.arange(DH)[None, None, :] == chosen[:, :, None]
    amplitude = jax.random.uniform(keys_split[1], head_shape, jnp.float32, 1.0, 4.0)
    cold_part = jnp.clip(-5.5 + 0.25 * jax.random.normal(keys_split[2], head_shape, jnp.float32), -6.0, -5.0)
    query_draw = jnp.clip(jax.random.normal(keys_split[3], head_shape, jnp.float32), -4.0, 4.0)
    key_draw = jnp.where(hot_mask, amplitude, cold_part)
    return (query_draw.reshape(TOKENS, HEAD_TOTAL * DH), key_draw.reshape(TOKENS, HEAD_TOTAL * DH))


def draw_queries(key, part):
    return query_key_couple(key)[0].astype(jnp.bfloat16)


def draw_keys(key, part):
    return query_key_couple(key)[1].astype(jnp.bfloat16)


def draw_decay(key, part):
    every_key_row = jax.random.split(jax.random.fold_in(key, 23), 5)
    fast_level = 4
    fast_heads = jax.random.randint(every_key_row[0], (HEAD_TOTAL,), 0, 8) < fast_level
    slow_rate = jnp.exp(jnp.log(0.5) / SEGMENT_TOTAL * jax.random.uniform(every_key_row[1], (SEGMENT_TOTAL, HEAD_TOTAL), jnp.float32, 0.5, 1.5))
    fast_rate = jax.random.uniform(every_key_row[2], (SEGMENT_TOTAL, HEAD_TOTAL), jnp.float32, 0.1, 0.4)
    decay_speed = jnp.where(fast_heads[None, :], fast_rate, slow_rate)
    sudden_spike = jax.random.randint(every_key_row[3], (SEGMENT_TOTAL, 1), 0, SEGMENT_TOTAL) < 3
    spike_factor = jax.random.uniform(every_key_row[4], (SEGMENT_TOTAL, HEAD_TOTAL), jnp.float32, 0.5, 0.8)
    return jnp.where(sudden_spike, decay_speed * spike_factor, decay_speed).astype(jnp.float32)


def block_levels(rng, dims, cuts, smallest, high):
    loudness = 1.0
    for axis_at, blocks in cuts:
        draws = jax.random.uniform(jax.random.fold_in(jax.random.fold_in(rng, 6), axis_at), (blocks,), jnp.float32, smallest / len(cuts), high / len(cuts))
        loudness = loudness * jnp.repeat(jnp.exp(draws), dims[axis_at] // blocks).reshape((-1,) + (1,) * (len(dims) - 1 - axis_at))
    return loudness


def normal_values(rng, extent, scale, bound, shards=(), kind=jnp.bfloat16):
    loudness = block_levels(rng, extent, shards, -0.22, 0.18) if shards else 1.0
    drawn = jax.random.normal(rng, extent, jnp.float32) * scale * loudness
    return jnp.minimum(jnp.maximum(drawn, -bound), bound).astype(kind)


def setup_inputs(seed: int = 0, part: int = 0) -> dict:
    streams_of = jax.random.split(jax.random.key(seed), 9)
    part_keys = jax.random.split(jax.random.fold_in(streams_of[8], part), 9)
    return {
        "queries": draw_queries(jax.random.fold_in(jax.random.fold_in(streams_of[8], part), 71), part),
        "keys": draw_keys(jax.random.fold_in(jax.random.fold_in(streams_of[8], part), 71), part),
        "values": normal_values(part_keys[2], (TOKENS, HEAD_TOTAL * DH), 1.0, 6.0, ((0, 4), (1, 4))),
        "decay": draw_decay(jax.random.fold_in(jax.random.fold_in(streams_of[8], part), 71), part),
        "gate": jnp.clip(-0.5 + 3.5 * jax.random.uniform(streams_of[4], (HEAD_TOTAL,), jnp.float32) ** block_levels(streams_of[4], (HEAD_TOTAL,), ((0, 4),), -0.2, 0.2), -0.5, 3.0),
        "summary": normal_values(part_keys[5], (SUMROWS, D), 1.0, 6.0, ((0, 4),)),
        "wq_sum": normal_values(streams_of[6], (D, HEAD_TOTAL * DH), (D // 4) ** -0.5, 0.25, ((1, 4),)),
        "wo_sum": normal_values(streams_of[7], (HEAD_TOTAL * DH, D), (HEAD_TOTAL * DH) ** -0.5, 0.125, ((0, 4),)),
    }


top_precision = lax.Precision.HIGHEST

def feature_map(inputs):
    return jax.nn.elu(inputs) + 1.0

def head_rms(inputs):
    return inputs * lax.rsqrt(lax.optimization_barrier(jnp.mean(inputs * inputs, axis=-1, keepdims=True)) + 1e-06)

def memory_read(lifted, memory, normalizer):
    numerator = jnp.einsum('qhd,hde->qhe', lifted, memory, precision=top_precision)
    denominator = jnp.einsum('qhd,hd->qh', lifted, normalizer, precision=top_precision) + 1.0
    return numerator / denominator[..., None]

def plain_attention(q_part, k_part, v_part):
    length = q_part.shape[0]
    scores = jnp.einsum('qhd,khd->hqk', q_part.astype(jnp.float32), k_part.astype(jnp.float32)) * q_part.shape[2] ** (-0.5)
    positions = jnp.arange(length)
    scores = jnp.where(positions[None, None, :] <= positions[None, :, None], scores, -jnp.inf)
    weights = jax.nn.softmax(scores, axis=-1).astype(jnp.bfloat16)
    return jnp.einsum('hqk,khd->qhd', weights.astype(jnp.float32), v_part.astype(jnp.float32))

def reference(queries, keys, values, decay, gate, summary, wq_sum, wo_sum):
    q_seg = queries.reshape(SEGMENT_TOTAL, SEG, HEAD_TOTAL, DH)
    k_seg = keys.reshape(SEGMENT_TOTAL, SEG, HEAD_TOTAL, DH)
    v_seg = values.reshape(SEGMENT_TOTAL, SEG, HEAD_TOTAL, DH)
    blend_weight = jax.nn.sigmoid(gate)[None, :, None]

    def one_segment(running, inputs_now):
        memory, normalizer = running
        q_part, k_part, v_part, seg_decay = inputs_now
        recalled = memory_read(feature_map(q_part.astype(jnp.float32)), memory, normalizer)
        local_out = plain_attention(q_part, k_part, v_part)
        mixed = head_rms(blend_weight * recalled + (1.0 - blend_weight) * local_out).astype(jnp.bfloat16)
        lifted_keys = feature_map(k_part.astype(jnp.float32))
        update = jnp.einsum('qhd,qhe->hde', lifted_keys, v_part.astype(jnp.float32), precision=top_precision)
        memory = seg_decay[:, None, None] * memory + update
        normalizer = seg_decay[:, None] * normalizer + lax.optimization_barrier(jnp.sum(lifted_keys, axis=0))
        return ((memory, normalizer), mixed)
    start_state = (jnp.zeros((HEAD_TOTAL, DH, DH), jnp.float32), jnp.zeros((HEAD_TOTAL, DH), jnp.float32))
    (final_memory, final_norm), attended = lax.scan(one_segment, start_state, (q_seg, k_seg, v_seg, decay))
    attended = attended.reshape(TOKENS, HEAD_TOTAL * DH)
    summary_state = summary
    row_count = summary.shape[0]
    for decode_step in range(STEPS):
        lifted = feature_map(jnp.dot(summary_state, wq_sum, preferred_element_type=jnp.float32).reshape(row_count, HEAD_TOTAL, DH))
        recalled = head_rms(memory_read(lifted, final_memory, final_norm)).astype(jnp.bfloat16)
        update = jnp.dot(recalled.reshape(row_count, HEAD_TOTAL * DH), wo_sum, preferred_element_type=jnp.float32)
        summary_state = (summary_state.astype(jnp.float32) + update).astype(jnp.bfloat16)
    return (attended, summary_state)
```

```python
import functools

import jax
import jax.numpy as jnp
from jax import lax
from jax.experimental import pallas as pl
from jax.experimental.pallas import tpu as pltpu
from jax.sharding import PartitionSpec as P

STEPS = 4
DH = 256
BLOCK = 256
LOG2E = 1.4426950408889634
F32 = jnp.float32
BF16 = jnp.bfloat16


def phi(x):
    return jnp.where(x > 0, x + 1.0, jnp.exp(jnp.minimum(x, 0.0)))


def rms(x):
    return x * lax.rsqrt(jnp.mean(x * x, axis=-1, keepdims=True) + 1e-06)


def kernel(
    ns, nz, heads,
    decay_ref, gate_ref, summary_ref, q_hbm, k_hbm, v_hbm, wq_hbm, wo_hbm,
    out_ref, sum_ref,
    q_ref, k_ref, v_ref, wq_ref, wo_ref,
    local_ref, mem_out, mem_in, prior_out, prior, final, nrm,
    part, part_in, state,
    load_sem, mem_ss, mem_rs, fin_ss, fin_rs, pri_ss, pri_rs, nrm_ss, nrm_rs,
    rs_ss, rs_rs, ag_ss, ag_rs,
):
    tokens = q_ref.shape[0]
    width = heads * DH
    slice_rows = DH // ns
    cols = wo_ref.shape[1] // nz
    me_s = lax.axis_index("seq")
    me_z = lax.axis_index("sub")

    loads = [
        pltpu.make_async_copy(src, dst, load_sem.at[i])
        for i, (src, dst) in enumerate(
            ((k_hbm, k_ref), (v_hbm, v_ref), (q_hbm, q_ref), (wq_hbm, wq_ref), (wo_hbm, wo_ref))
        )
    ]
    for load in loads:
        load.start()

    barrier = pltpu.get_barrier_semaphore()
    for o in range(1, ns):
        pl.semaphore_signal(barrier, inc=1, device_id={"seq": lax.rem(me_s + o, ns)},
                            device_id_type=pl.DeviceIdType.MESH)
    for o in range(1, nz):
        pl.semaphore_signal(barrier, inc=1, device_id={"sub": lax.rem(me_z + o, nz)},
                            device_id_type=pl.DeviceIdType.MESH)
    pl.semaphore_wait(barrier, ns - 1 + nz - 1)

    def to(axis, target, src, dst, ss, rs):
        return pltpu.make_async_remote_copy(
            src_ref=src, dst_ref=dst, send_sem=ss, recv_sem=rs,
            device_id={axis: target}, device_id_type=pl.DeviceIdType.MESH)

    loads[0].wait()
    loads[1].wait()
    for h in range(heads):
        col = pl.ds(h * DH, DH)
        lifted = phi(k_ref[:, col].astype(F32))
        nrm[me_s, :, col] = jnp.broadcast_to(jnp.sum(lifted, axis=0, keepdims=True), (8, DH))
        update = lax.dot_general(lifted.astype(BF16), v_ref[:, col], (((0,), (0,)), ((), ())),
                                 preferred_element_type=F32).astype(BF16)
        mem_out[:, h] = update.reshape(ns, slice_rows, DH)

    mem_copies, nrm_copies = [], []
    for o in range(1, ns):
        target = lax.rem(me_s + o, ns)
        mem_copies.append(to("seq", target, mem_out.at[target], mem_in.at[me_s],
                             mem_ss.at[o - 1], mem_rs.at[o - 1]))
        nrm_copies.append(to("seq", target, nrm.at[me_s], nrm.at[me_s],
                             nrm_ss.at[o - 1], nrm_rs.at[o - 1]))
    for copy in mem_copies + nrm_copies:
        copy.start()
    mem_in[me_s] = mem_out[me_s]

    scale = DH ** (-0.5) * LOG2E

    def attend(block, h):
        rows = pl.ds(block * BLOCK, BLOCK)
        col = pl.ds(h * DH, DH)
        span = (block + 1) * BLOCK
        scores = lax.dot_general(q_ref[rows, col], k_ref[pl.ds(0, span), col],
                                 (((1,), (1,)), ((), ())), preferred_element_type=F32)
        at_row = lax.broadcasted_iota(jnp.int32, (BLOCK, BLOCK), 0)
        at_col = lax.broadcasted_iota(jnp.int32, (BLOCK, BLOCK), 1)
        last = jnp.where(at_col <= at_row, scores[:, span - BLOCK:], -jnp.inf)
        if block:
            scores = jnp.concatenate([scores[:, : span - BLOCK], last], axis=1)
        else:
            scores = last
        top = jnp.max(scores, axis=1, keepdims=True)
        weights = jnp.exp2((scores - top) * scale)
        total = jnp.sum(weights, axis=1, keepdims=True)
        mixed = jnp.dot(weights.astype(BF16), v_ref[pl.ds(0, span), col],
                        preferred_element_type=F32)
        local_ref[rows, col] = mixed / total

    def finish(block, h, prior_norm):
        rows = pl.ds(block * BLOCK, BLOCK)
        col = pl.ds(h * DH, DH)
        lifted = phi(q_ref[rows, col].astype(F32))
        below = jnp.sum(lifted * prior_norm[:, h * DH:(h + 1) * DH], axis=1, keepdims=True) + 1.0
        above = jnp.dot(lifted.astype(BF16), prior[:, h].reshape(DH, DH),
                        preferred_element_type=F32)
        blend = 1.0 / (1.0 + jnp.exp(-jnp.full((1, DH), gate_ref[h], F32)))
        mixed = blend * (above / below) + (1.0 - blend) * local_ref[rows, col]
        out_ref[rows, col] = rms(mixed).astype(BF16)

    blocks = tokens // BLOCK
    units = []
    for h in range(heads):
        for i in range((blocks + 1) // 2):
            units.append([(b, h) for b in sorted({blocks - 1 - i, i}, reverse=True)])
    phases = 2 + 2 * STEPS
    early = 3
    plan = [[] for _ in range(phases)]
    for i, unit in enumerate(units):
        at = i * 8 // len(units)
        plan[at] += [("attend", pair) for pair in unit]
        if at < early:
            plan[8 + (at == early - 1)] += [("finish", pair) for pair in unit]
        else:
            plan[at] += [("finish", pair) for pair in unit]

    ready = {}

    def work(phase):
        for what, (block, h) in plan[phase]:
            if what == "attend":
                attend(block, h)
            else:
                finish(block, h, ready["prior_norm"])

    loads[2].wait()
    work(0)

    for copy in mem_copies:
        copy.wait()
    for h in range(heads):
        running = jnp.zeros((slice_rows, DH), F32)
        for s in range(ns):
            prior_out[s, h] = running.astype(BF16)
            running = decay_ref[s, h] * running + mem_in[s, h].astype(F32)
        final[me_s, h] = running.astype(BF16)
    fin_copies, pri_copies = [], []
    for o in range(1, ns):
        target = lax.rem(me_s + o, ns)
        fin_copies.append(to("seq", target, final.at[me_s], final.at[me_s],
                             fin_ss.at[o - 1], fin_rs.at[o - 1]))
        pri_copies.append(to("seq", target, prior_out.at[target], prior.at[me_s],
                             pri_ss.at[o - 1], pri_rs.at[o - 1]))
    for copy in fin_copies + pri_copies:
        copy.start()
    prior[me_s] = prior_out[me_s]

    work(1)

    for copy in nrm_copies:
        copy.wait()
    prior_parts, final_parts = [], []
    for h in range(heads):
        running = jnp.zeros((1, DH), F32)
        before = running
        for s in range(ns):
            before = jnp.where(me_s == s, running, before)
            running = decay_ref[s, h] * running + nrm[s, 0:1, h * DH:(h + 1) * DH]
        prior_parts.append(before)
        final_parts.append(running)
    ready["prior_norm"] = jnp.concatenate(prior_parts, axis=1)

    for copy in fin_copies:
        copy.wait()

    for o in range(nz):
        source = lax.rem(me_z + nz - o, nz)
        state[o] = summary_ref[:, pl.ds(pl.multiple_of(source * cols, cols), cols)]
    loads[3].wait()
    loads[4].wait()
    for step in range(STEPS):
        lifted = None
        for o in range(nz):
            source = lax.rem(me_z + nz - o, nz)
            rows = pl.ds(pl.multiple_of(source * cols, cols), cols)
            term = jnp.dot(state[o], wq_ref[rows, :], preferred_element_type=F32)
            lifted = term if lifted is None else lifted + term
        lifted = phi(lifted)
        reads = []
        for h in range(heads):
            mine = lifted[:, h * DH:(h + 1) * DH]
            below = jnp.sum(mine * final_parts[h], axis=1, keepdims=True) + 1.0
            above = jnp.dot(mine.astype(BF16), final[:, h].reshape(DH, DH),
                            preferred_element_type=F32)
            reads.append(rms(above / below).astype(BF16))
        read = jnp.concatenate(reads, axis=1) if heads > 1 else reads[0]
        copies = []
        for o in range(1, nz):
            target = lax.rem(me_z + o, nz)
            there = pl.ds(pl.multiple_of(target * cols, cols), cols)
            part[o - 1] = jnp.dot(read, wo_ref[:, there], preferred_element_type=F32).astype(BF16)
            copy = to("sub", target, part.at[o - 1], part_in.at[o - 1],
                      rs_ss.at[o - 1], rs_rs.at[o - 1])
            copy.start()
            copies.append(copy)
        here = pl.ds(pl.multiple_of(me_z * cols, cols), cols)
        total = jnp.dot(read, wo_ref[:, here], preferred_element_type=F32)

        if step == 0:
            work(2)
            for copy in pri_copies:
                copy.wait()
        else:
            work(2 + 2 * step)

        for copy in copies:
            copy.wait()
        for o in range(1, nz):
            total = total + part_in[o - 1].astype(F32)
        state[0] = (state[0].astype(F32) + total).astype(BF16)
        copies = []
        for o in range(1, nz):
            target = lax.rem(me_z + o, nz)
            copy = to("sub", target, state.at[0], state.at[o], ag_ss.at[o - 1], ag_rs.at[o - 1])
            copy.start()
            copies.append(copy)
        work(3 + 2 * step)
        for copy in copies:
            copy.wait()
    for o in range(nz):
        source = lax.rem(me_z + nz - o, nz)
        sum_ref[:, pl.ds(pl.multiple_of(source * cols, cols), cols)] = state[o]


def on_device(queries, keys, values, decay, gate, summary, wq_sum, wo_sum):
    ns, nz = lax.axis_size("seq"), lax.axis_size("sub")
    heads = gate.shape[0]
    tokens, width = queries.shape
    rows, model = summary.shape
    cols = model // nz
    slice_rows = DH // ns
    whole = pl.BlockSpec(memory_space=pltpu.VMEM)
    scalars = pl.BlockSpec(memory_space=pltpu.SMEM)
    anywhere = pl.BlockSpec(memory_space=pl.ANY)
    sems = lambda count: pltpu.SemaphoreType.DMA((count,))
    return pl.pallas_call(
        functools.partial(kernel, ns, nz, heads),
        out_shape=(
            jax.ShapeDtypeStruct((tokens, width), BF16),
            jax.ShapeDtypeStruct((rows, model), BF16),
        ),
        in_specs=[scalars, scalars, whole] + [anywhere] * 5,
        out_specs=(whole, whole),
        scratch_shapes=[
            pltpu.VMEM((tokens, width), BF16),
            pltpu.VMEM((tokens, width), BF16),
            pltpu.VMEM((tokens, width), BF16),
            pltpu.VMEM((model, width), BF16),
            pltpu.VMEM((width, model), BF16),
            pltpu.VMEM((tokens, width), F32),
            pltpu.VMEM((ns, heads, slice_rows, DH), BF16),
            pltpu.VMEM((ns, heads, slice_rows, DH), BF16),
            pltpu.VMEM((ns, heads, slice_rows, DH), BF16),
            pltpu.VMEM((ns, heads, slice_rows, DH), BF16),
            pltpu.VMEM((ns, heads, slice_rows, DH), BF16),
            pltpu.VMEM((ns, 8, width), F32),
            pltpu.VMEM((nz - 1, rows, cols), BF16),
            pltpu.VMEM((nz - 1, rows, cols), BF16),
            pltpu.VMEM((nz, rows, cols), BF16),
            sems(5),
            sems(ns - 1), sems(ns - 1), sems(ns - 1), sems(ns - 1),
            sems(ns - 1), sems(ns - 1), sems(ns - 1), sems(ns - 1),
            sems(nz - 1), sems(nz - 1), sems(nz - 1), sems(nz - 1),
        ],
        compiler_params=pltpu.CompilerParams(
            collective_id=0, has_side_effects=True, vmem_limit_bytes=56 * 1024 * 1024
        ),
        cost_estimate=pl.CostEstimate(
            flops=7 * 10**9, bytes_accessed=12 * 2**20, transcendentals=6 * 10**6
        ),
    )(decay, gate, summary, queries, keys, values, wq_sum, wo_sum)


def solution(mesh):
    placed = (
        P(("book", "seq"), "sub"),
        P(("book", "seq"), "sub"),
        P(("book", "seq"), "sub"),
        P("book", "sub"),
        P("sub"),
        P(("book", "seq"), None),
        P(None, "sub"),
        P("sub", None),
    )
    return jax.shard_map(
        on_device,
        mesh=mesh,
        in_specs=placed,
        out_specs=(P(("book", "seq"), "sub"), P(("book", "seq"), None)),
        check_vma=False,
    )
```

```python
import functools

import jax
import jax.numpy as jnp
from jax import lax
from jax.experimental import pallas as pl
from jax.experimental.pallas import tpu as pltpu
from jax.sharding import PartitionSpec as P

STEPS = 4
DH = 256
BLOCK = 256
LOG2E = 1.4426950408889634
F32 = jnp.float32
BF16 = jnp.bfloat16


def phi(x):
    return jnp.where(x > 0, x + 1.0, jnp.exp(jnp.minimum(x, 0.0)))


def rms(x):
    return x * lax.rsqrt(jnp.mean(x * x, axis=-1, keepdims=True) + 1e-06)


def kernel(
    ns, nz, heads,
    decay_ref, gate_ref, summary_ref, q_hbm, k_hbm, v_hbm, wq_hbm, wo_hbm,
    out_hbm, sum_ref,
    q_ref, k_ref, v_ref, wq_ref, wo_ref,
    local_ref, mem_out, mem_in, prior_out, prior, final, nrm,
    part, part_in, state, out_ref,
    load_sem, out_sem, mem_ss, mem_rs, fin_ss, fin_rs, pri_ss, pri_rs, nrm_ss, nrm_rs,
    rs_ss, rs_rs, ag_ss, ag_rs,
):
    tokens = q_ref.shape[0]
    width = heads * DH
    slice_rows = DH // ns
    cols = wo_ref.shape[1] // nz
    blocks = tokens // BLOCK
    out_copies = []
    me_s = lax.axis_index("seq")
    me_z = lax.axis_index("sub")

    def load(i, src, dst):
        return pltpu.make_async_copy(src, dst, load_sem.at[i])

    early_loads = []
    for h in range(heads):
        col = pl.ds(h * DH, DH)
        early_loads.append((load(2 * h, k_hbm.at[:, col], k_ref.at[:, col]),
                            load(2 * h + 1, v_hbm.at[:, col], v_ref.at[:, col])))
    for pair in early_loads:
        for one in pair:
            one.start()
    late_loads = [load(2 * heads, q_hbm, q_ref), load(2 * heads + 1, wq_hbm, wq_ref),
                  load(2 * heads + 2, wo_hbm, wo_ref)]

    barrier = pltpu.get_barrier_semaphore()
    for o in range(1, ns):
        pl.semaphore_signal(barrier, inc=1, device_id={"seq": lax.rem(me_s + o, ns)},
                            device_id_type=pl.DeviceIdType.MESH)
    for o in range(1, nz):
        pl.semaphore_signal(barrier, inc=1, device_id={"sub": lax.rem(me_z + o, nz)},
                            device_id_type=pl.DeviceIdType.MESH)
    pl.semaphore_wait(barrier, ns - 1 + nz - 1)

    def to(axis, target, src, dst, ss, rs):
        return pltpu.make_async_remote_copy(
            src_ref=src, dst_ref=dst, send_sem=ss, recv_sem=rs,
            device_id={axis: target}, device_id_type=pl.DeviceIdType.MESH)

    for h in range(heads):
        for one in early_loads[h]:
            one.wait()
        if h == heads - 1:
            for one in late_loads:
                one.start()
        col = pl.ds(h * DH, DH)
        lifted = phi(k_ref[:, col].astype(F32))
        nrm[me_s, :, col] = jnp.broadcast_to(jnp.sum(lifted, axis=0, keepdims=True), (8, DH))
        update = lax.dot_general(lifted.astype(BF16), v_ref[:, col], (((0,), (0,)), ((), ())),
                                 preferred_element_type=F32).astype(BF16)
        mem_out[:, h] = update.reshape(ns, slice_rows, DH)

    mem_copies, nrm_copies = [], []
    for o in range(1, ns):
        target = lax.rem(me_s + o, ns)
        mem_copies.append(to("seq", target, mem_out.at[target], mem_in.at[me_s],
                             mem_ss.at[o - 1], mem_rs.at[o - 1]))
        nrm_copies.append(to("seq", target, nrm.at[me_s], nrm.at[me_s],
                             nrm_ss.at[o - 1], nrm_rs.at[o - 1]))
    for copy in mem_copies + nrm_copies:
        copy.start()
    mem_in[me_s] = mem_out[me_s]

    scale = DH ** (-0.5) * LOG2E

    def attend(block, h):
        rows = pl.ds(block * BLOCK, BLOCK)
        col = pl.ds(h * DH, DH)
        span = (block + 1) * BLOCK
        scores = lax.dot_general(q_ref[rows, col], k_ref[pl.ds(0, span), col],
                                 (((1,), (1,)), ((), ())), preferred_element_type=F32)
        at_row = lax.broadcasted_iota(jnp.int32, (BLOCK, BLOCK), 0)
        at_col = lax.broadcasted_iota(jnp.int32, (BLOCK, BLOCK), 1)
        last = jnp.where(at_col <= at_row, scores[:, span - BLOCK:], -jnp.inf)
        if block:
            scores = jnp.concatenate([scores[:, : span - BLOCK], last], axis=1)
        else:
            scores = last
        top = jnp.max(scores, axis=1, keepdims=True)
        weights = jnp.exp2((scores - top) * scale)
        total = jnp.sum(weights, axis=1, keepdims=True)
        mixed = jnp.dot(weights.astype(BF16), v_ref[pl.ds(0, span), col],
                        preferred_element_type=F32)
        local_ref[rows, col] = mixed / total

    def finish(block, h, prior_norm):
        rows = pl.ds(block * BLOCK, BLOCK)
        col = pl.ds(h * DH, DH)
        lifted = phi(q_ref[rows, col].astype(F32))
        below = jnp.sum(lifted * prior_norm[:, h * DH:(h + 1) * DH], axis=1, keepdims=True) + 1.0
        above = jnp.dot(lifted.astype(BF16), prior[:, h].reshape(DH, DH),
                        preferred_element_type=F32)
        blend = 1.0 / (1.0 + jnp.exp(-jnp.full((1, DH), gate_ref[h], F32)))
        mixed = blend * (above / below) + (1.0 - blend) * local_ref[rows, col]
        out_ref[rows, col] = rms(mixed).astype(BF16)
        copy = pltpu.make_async_copy(out_ref.at[rows, col], out_hbm.at[rows, col],
                                     out_sem.at[h * blocks + block])
        copy.start()
        out_copies.append(copy)

    order = []
    for h in range(heads):
        for i in range((blocks + 1) // 2):
            order += [(b, h) for b in sorted({blocks - 1 - i, i}, reverse=True)]
    weights = [2, 2] + [1] * (4 * STEPS)
    first_finish = 4
    total_cost = sum(block + 2 for block, _ in order)
    plan = []
    spent, deferred = 0, []
    for phase in range(len(weights)):
        aim = total_cost * sum(weights[: phase + 1]) / sum(weights)
        now = []
        while (order or (deferred and phase >= first_finish)) and (
            spent < aim or phase == len(weights) - 1
        ):
            if order:
                block, h = order.pop(0)
                now.append(("attend", block, h))
                spent += block + 1
                if phase >= first_finish:
                    now.append(("finish", block, h))
                    spent += 1
                else:
                    deferred.append((block, h))
            else:
                block, h = deferred.pop(0)
                now.append(("finish", block, h))
                spent += 1
        plan.append(now)
    plan = iter(plan)
    ready = {}

    def work():
        for what, block, h in next(plan):
            if what == "attend":
                attend(block, h)
            else:
                if "prior" not in ready:
                    for copy in pri_copies:
                        copy.wait()
                    ready["prior"] = True
                finish(block, h, ready["prior_norm"])

    late_loads[0].wait()
    work()

    for copy in mem_copies:
        copy.wait()
    for h in range(heads):
        running = jnp.zeros((slice_rows, DH), F32)
        for s in range(ns):
            prior_out[s, h] = running.astype(BF16)
            running = decay_ref[h, s] * running + mem_in[s, h].astype(F32)
        final[me_s, h] = running.astype(BF16)
    fin_copies, pri_copies = [], []
    for o in range(1, ns):
        target = lax.rem(me_s + o, ns)
        fin_copies.append(to("seq", target, final.at[me_s], final.at[me_s],
                             fin_ss.at[o - 1], fin_rs.at[o - 1]))
        pri_copies.append(to("seq", target, prior_out.at[target], prior.at[me_s],
                             pri_ss.at[o - 1], pri_rs.at[o - 1]))
    for copy in fin_copies + pri_copies:
        copy.start()
    prior[me_s] = prior_out[me_s]

    work()

    for copy in nrm_copies:
        copy.wait()
    prior_parts, final_parts = [], []
    for h in range(heads):
        running = jnp.zeros((1, DH), F32)
        before = running
        for s in range(ns):
            before = jnp.where(me_s == s, running, before)
            running = decay_ref[h, s] * running + nrm[s, 0:1, h * DH:(h + 1) * DH]
        prior_parts.append(before)
        final_parts.append(running)
    ready["prior_norm"] = jnp.concatenate(prior_parts, axis=1)

    half = sum_ref.shape[0] // 2

    def columns(index):
        return pl.ds(pl.multiple_of(index * cols, cols), cols)

    def project(g):
        total = None
        for o in range(nz):
            source = lax.rem(me_z + nz - o, nz)
            term = jnp.dot(state[g, o], wq_ref[columns(source), :], preferred_element_type=F32)
            total = term if total is None else total + term
        return total

    def read_and_scatter(g, projected):
        lifted = phi(projected)
        reads = []
        for h in range(heads):
            mine = lifted[:, h * DH:(h + 1) * DH]
            below = jnp.sum(mine * final_parts[h], axis=1, keepdims=True) + 1.0
            above = jnp.dot(mine.astype(BF16), final[:, h].reshape(DH, DH),
                            preferred_element_type=F32)
            reads.append(rms(above / below).astype(BF16))
        read = jnp.concatenate(reads, axis=1) if heads > 1 else reads[0]
        copies = []
        for o in range(1, nz):
            target = lax.rem(me_z + o, nz)
            part[g, o - 1] = jnp.dot(read, wo_ref[:, columns(target)],
                                     preferred_element_type=F32).astype(BF16)
            copy = to("sub", target, part.at[g, o - 1], part_in.at[g, o - 1],
                      rs_ss.at[g, o - 1], rs_rs.at[g, o - 1])
            copy.start()
            copies.append(copy)
        own = jnp.dot(read, wo_ref[:, columns(me_z)], preferred_element_type=F32)
        return copies, own

    def reduce_and_gather(g, copies, total):
        for copy in copies:
            copy.wait()
        for o in range(1, nz):
            total = total + part_in[g, o - 1].astype(F32)
        state[g, 0] = (state[g, 0].astype(F32) + total).astype(BF16)
        gathers = []
        for o in range(1, nz):
            target = lax.rem(me_z + o, nz)
            copy = to("sub", target, state.at[g, 0], state.at[g, o],
                      ag_ss.at[g, o - 1], ag_rs.at[g, o - 1])
            copy.start()
            gathers.append(copy)
        return gathers

    for g in range(2):
        for o in range(nz):
            source = lax.rem(me_z + nz - o, nz)
            state[g, o] = summary_ref[pl.ds(g * half, half), columns(source)]
    late_loads[1].wait()
    projected = [project(g) for g in range(2)]
    late_loads[2].wait()
    for copy in fin_copies:
        copy.wait()
    scatters = [read_and_scatter(g, projected[g]) for g in range(2)]
    for step in range(STEPS):
        gathers = []
        for g in range(2):
            work()
            gathers.append(reduce_and_gather(g, *scatters[g]))
        for g in range(2):
            work()
            for copy in gathers[g]:
                copy.wait()
            if step < STEPS - 1:
                scatters[g] = read_and_scatter(g, project(g))
    for g in range(2):
        for o in range(nz):
            source = lax.rem(me_z + nz - o, nz)
            sum_ref[pl.ds(g * half, half), columns(source)] = state[g, o]
    for copy in out_copies:
        copy.wait()


def hand_on_kernel(attended, summarized, attended_out, summarized_out, sem):
    rows = attended.shape[0] // 4
    copies = [pltpu.make_async_copy(summarized, summarized_out, sem.at[4])]
    for i in range(4):
        piece = pl.ds(i * rows, rows)
        copies.append(pltpu.make_async_copy(attended.at[piece], attended_out.at[piece], sem.at[i]))
    for copy in copies:
        copy.start()
    for copy in copies:
        copy.wait()


def on_device(queries, keys, values, decay, gate, summary, wq_sum, wo_sum):
    ns, nz = lax.axis_size("seq"), lax.axis_size("sub")
    heads = gate.shape[0]
    tokens, width = queries.shape
    rows, model = summary.shape
    cols = model // nz
    slice_rows = DH // ns
    whole = pl.BlockSpec(memory_space=pltpu.VMEM)
    scalars = pl.BlockSpec(memory_space=pltpu.SMEM)
    anywhere = pl.BlockSpec(memory_space=pl.ANY)
    sems = lambda *count: pltpu.SemaphoreType.DMA(count)
    half = rows // 2
    results = pl.pallas_call(
        functools.partial(kernel, ns, nz, heads),
        out_shape=(
            jax.ShapeDtypeStruct((tokens, width), BF16),
            jax.ShapeDtypeStruct((rows, model), BF16),
        ),
        in_specs=[scalars, scalars, whole] + [anywhere] * 5,
        out_specs=(anywhere, whole),
        scratch_shapes=[
            pltpu.VMEM((tokens, width), BF16),
            pltpu.VMEM((tokens, width), BF16),
            pltpu.VMEM((tokens, width), BF16),
            pltpu.VMEM((model, width), BF16),
            pltpu.VMEM((width, model), BF16),
            pltpu.VMEM((tokens, width), F32),
            pltpu.VMEM((ns, heads, slice_rows, DH), BF16),
            pltpu.VMEM((ns, heads, slice_rows, DH), BF16),
            pltpu.VMEM((ns, heads, slice_rows, DH), BF16),
            pltpu.VMEM((ns, heads, slice_rows, DH), BF16),
            pltpu.VMEM((ns, heads, slice_rows, DH), BF16),
            pltpu.VMEM((ns, 8, width), F32),
            pltpu.VMEM((2, nz - 1, half, cols), BF16),
            pltpu.VMEM((2, nz - 1, half, cols), BF16),
            pltpu.VMEM((2, nz, half, cols), BF16),
            pltpu.VMEM((tokens, width), BF16),
            sems(2 * heads + 3),
            sems(heads * tokens // BLOCK),
            sems(ns - 1), sems(ns - 1), sems(ns - 1), sems(ns - 1),
            sems(ns - 1), sems(ns - 1), sems(ns - 1), sems(ns - 1),
            sems(2, nz - 1), sems(2, nz - 1), sems(2, nz - 1), sems(2, nz - 1),
        ],
        compiler_params=pltpu.CompilerParams(
            collective_id=0, has_side_effects=True, vmem_limit_bytes=56 * 1024 * 1024
        ),
        cost_estimate=pl.CostEstimate(
            flops=7 * 10**9, bytes_accessed=12 * 2**20, transcendentals=6 * 10**6
        ),
    )(decay.T, gate, summary, queries, keys, values, wq_sum, wo_sum)
    return pl.pallas_call(
        hand_on_kernel,
        out_shape=tuple(jax.ShapeDtypeStruct(x.shape, x.dtype) for x in results),
        in_specs=[anywhere] * 2,
        out_specs=(anywhere, anywhere),
        scratch_shapes=[sems(5)],
        compiler_params=pltpu.CompilerParams(vmem_limit_bytes=56 * 1024 * 1024),
    )(*results)


def solution(mesh):
    placed = (
        P(("book", "seq"), "sub"),
        P(("book", "seq"), "sub"),
        P(("book", "seq"), "sub"),
        P("book", "sub"),
        P("sub"),
        P(("book", "seq"), None),
        P(None, "sub"),
        P("sub", None),
    )
    return jax.shard_map(
        on_device,
        mesh=mesh,
        in_specs=placed,
        out_specs=(P(("book", "seq"), "sub"), P(("book", "seq"), None)),
        check_vma=False,
    )
```

```python
import functools

import jax
import jax.numpy as jnp
from jax import lax
from jax.experimental import pallas as pl
from jax.experimental.pallas import tpu as pltpu
from jax.sharding import PartitionSpec as P

STEPS = 4
DH = 256
BLOCK = 256
LOG2E = 1.4426950408889634
F32 = jnp.float32
BF16 = jnp.bfloat16


def phi(x):
    return jnp.where(x > 0, x + 1.0, jnp.exp(jnp.minimum(x, 0.0)))


def rms(x):
    return x * lax.rsqrt(jnp.mean(x * x, axis=-1, keepdims=True) + 1e-06)


def kernel(
    ns, nz, heads,
    decay_ref, gate_ref, summary_ref, q_hbm, k_hbm, v_hbm, wq_hbm, wo_hbm,
    out_ref, sum_ref,
    q_ref, k_ref, v_ref, wq_ref, wo_ref,
    local_ref, mem_out, mem_in, prior_out, prior, final, nrm,
    part, part_in, state,
    load_sem, mem_ss, mem_rs, fin_ss, fin_rs, pri_ss, pri_rs, nrm_ss, nrm_rs,
    rs_ss, rs_rs, ag_ss, ag_rs,
):
    tokens = q_ref.shape[0]
    width = heads * DH
    slice_rows = DH // ns
    cols = wo_ref.shape[1] // nz
    blocks = tokens // BLOCK
    me_s = lax.axis_index("seq")
    me_z = lax.axis_index("sub")

    def load(i, src, dst):
        return pltpu.make_async_copy(src, dst, load_sem.at[i])

    early_loads = []
    for h in range(heads):
        col = pl.ds(h * DH, DH)
        early_loads.append((load(2 * h, k_hbm.at[:, col], k_ref.at[:, col]),
                            load(2 * h + 1, v_hbm.at[:, col], v_ref.at[:, col])))
    for pair in early_loads:
        for one in pair:
            one.start()
    late_loads = [load(2 * heads, q_hbm, q_ref), load(2 * heads + 1, wq_hbm, wq_ref),
                  load(2 * heads + 2, wo_hbm, wo_ref)]

    barrier = pltpu.get_barrier_semaphore()
    for o in range(1, ns):
        pl.semaphore_signal(barrier, inc=1, device_id={"seq": lax.rem(me_s + o, ns)},
                            device_id_type=pl.DeviceIdType.MESH)
    for o in range(1, nz):
        pl.semaphore_signal(barrier, inc=1, device_id={"sub": lax.rem(me_z + o, nz)},
                            device_id_type=pl.DeviceIdType.MESH)
    pl.semaphore_wait(barrier, ns - 1 + nz - 1)

    def to(axis, target, src, dst, ss, rs):
        return pltpu.make_async_remote_copy(
            src_ref=src, dst_ref=dst, send_sem=ss, recv_sem=rs,
            device_id={axis: target}, device_id_type=pl.DeviceIdType.MESH)

    mem_copies = [[] for _ in range(heads)]
    for h in range(heads):
        for one in early_loads[h]:
            one.wait()
        if h == heads - 1:
            for one in late_loads:
                one.start()
        col = pl.ds(h * DH, DH)
        lifted = phi(k_ref[:, col].astype(F32))
        update = lax.dot_general(lifted.astype(BF16), v_ref[:, col], (((0,), (0,)), ((), ())),
                                 preferred_element_type=F32).astype(BF16)
        mem_out[:, h] = update.reshape(ns, slice_rows, DH)
        for o in range(1, ns):
            target = lax.rem(me_s + o, ns)
            copy = to("seq", target, mem_out.at[target, h], mem_in.at[me_s, h],
                      mem_ss.at[h, o - 1], mem_rs.at[h, o - 1])
            copy.start()
            mem_copies[h].append(copy)
        nrm[me_s, :, col] = jnp.broadcast_to(jnp.sum(lifted, axis=0, keepdims=True), (8, DH))
    nrm_copies = []
    for o in range(1, ns):
        target = lax.rem(me_s + o, ns)
        copy = to("seq", target, nrm.at[me_s], nrm.at[me_s], nrm_ss.at[o - 1], nrm_rs.at[o - 1])
        copy.start()
        nrm_copies.append(copy)
    mem_in[me_s] = mem_out[me_s]

    scale = DH ** (-0.5) * LOG2E

    def attend(block, h):
        rows = pl.ds(block * BLOCK, BLOCK)
        col = pl.ds(h * DH, DH)
        span = (block + 1) * BLOCK
        scores = lax.dot_general(q_ref[rows, col], k_ref[pl.ds(0, span), col],
                                 (((1,), (1,)), ((), ())), preferred_element_type=F32)
        at_row = lax.broadcasted_iota(jnp.int32, (BLOCK, BLOCK), 0)
        at_col = lax.broadcasted_iota(jnp.int32, (BLOCK, BLOCK), 1)
        last = jnp.where(at_col <= at_row, scores[:, span - BLOCK:], -jnp.inf)
        if block:
            scores = jnp.concatenate([scores[:, : span - BLOCK], last], axis=1)
        else:
            scores = last
        top = jnp.max(scores, axis=1, keepdims=True)
        weights = jnp.exp2((scores - top) * scale)
        total = jnp.sum(weights, axis=1, keepdims=True)
        mixed = jnp.dot(weights.astype(BF16), v_ref[pl.ds(0, span), col],
                        preferred_element_type=F32)
        local_ref[rows, col] = mixed / total

    def finish(block, h, prior_norm):
        rows = pl.ds(block * BLOCK, BLOCK)
        col = pl.ds(h * DH, DH)
        lifted = phi(q_ref[rows, col].astype(F32))
        below = jnp.sum(lifted * prior_norm[:, h * DH:(h + 1) * DH], axis=1, keepdims=True) + 1.0
        above = jnp.dot(lifted.astype(BF16), prior[:, h].reshape(DH, DH),
                        preferred_element_type=F32)
        blend = 1.0 / (1.0 + jnp.exp(-jnp.full((1, DH), gate_ref[h], F32)))
        mixed = blend * (above / below) + (1.0 - blend) * local_ref[rows, col]
        out_ref[rows, col] = rms(mixed).astype(BF16)

    order = []
    for h in range(heads):
        for i in range((blocks + 1) // 2):
            order += [(b, h) for b in sorted({blocks - 1 - i, i}, reverse=True)]
    weights = [8, 8] + [1, 4, 4, 1] * (STEPS - 1) + [1, 4, 4, 4]
    first_finish = 4
    total_cost = sum(block + 2 for block, _ in order)
    plan = []
    spent, deferred = 0, []
    for phase in range(len(weights)):
        aim = total_cost * sum(weights[: phase + 1]) / sum(weights)
        now = []
        while (order or (deferred and phase >= first_finish)) and (
            spent < aim or phase == len(weights) - 1
        ):
            if order:
                block, h = order.pop(0)
                now.append(("attend", block, h))
                spent += block + 1
                if phase >= first_finish:
                    now.append(("finish", block, h))
                    spent += 1
                else:
                    deferred.append((block, h))
            else:
                block, h = deferred.pop(0)
                now.append(("finish", block, h))
                spent += 1
        plan.append(now)
    plan = iter(plan)
    ready = {}

    def work():
        for what, block, h in next(plan):
            if what == "attend":
                attend(block, h)
            else:
                if "prior" not in ready:
                    for copy in pri_copies:
                        copy.wait()
                    ready["prior"] = True
                finish(block, h, ready["prior_norm"])

    late_loads[0].wait()
    work()

    fin_copies, pri_copies = [], []
    for h in range(heads):
        for copy in mem_copies[h]:
            copy.wait()
        running = jnp.zeros((slice_rows, DH), F32)
        for s in range(ns):
            prior_out[s, h] = running.astype(BF16)
            running = decay_ref[h, s] * running + mem_in[s, h].astype(F32)
        final[me_s, h] = running.astype(BF16)
        for o in range(1, ns):
            target = lax.rem(me_s + o, ns)
            copy = to("seq", target, final.at[me_s, h], final.at[me_s, h],
                      fin_ss.at[h, o - 1], fin_rs.at[h, o - 1])
            copy.start()
            fin_copies.append(copy)
    for o in range(1, ns):
        target = lax.rem(me_s + o, ns)
        copy = to("seq", target, prior_out.at[target], prior.at[me_s],
                  pri_ss.at[o - 1], pri_rs.at[o - 1])
        copy.start()
        pri_copies.append(copy)
    prior[me_s] = prior_out[me_s]

    work()

    for copy in nrm_copies:
        copy.wait()
    prior_parts, final_parts = [], []
    for h in range(heads):
        running = jnp.zeros((1, DH), F32)
        before = running
        for s in range(ns):
            before = jnp.where(me_s == s, running, before)
            running = decay_ref[h, s] * running + nrm[s, 0:1, h * DH:(h + 1) * DH]
        prior_parts.append(before)
        final_parts.append(running)
    ready["prior_norm"] = jnp.concatenate(prior_parts, axis=1)

    half = sum_ref.shape[0] // 2

    def columns(index):
        return pl.ds(pl.multiple_of(index * cols, cols), cols)

    others = sorted(range(1, nz), key=lambda o: abs(2 * o - nz))

    def project_chunk(g, o):
        source = lax.rem(me_z + nz - o, nz)
        return jnp.dot(state[g, o], wq_ref[columns(source), :], preferred_element_type=F32)

    def read_and_scatter(g, projected):
        lifted = phi(projected)
        reads = []
        for h in range(heads):
            mine = lifted[:, h * DH:(h + 1) * DH]
            below = jnp.sum(mine * final_parts[h], axis=1, keepdims=True) + 1.0
            above = jnp.dot(mine.astype(BF16), final[:, h].reshape(DH, DH),
                            preferred_element_type=F32)
            reads.append(rms(above / below).astype(BF16))
        read = jnp.concatenate(reads, axis=1) if heads > 1 else reads[0]
        copies = []
        for o in others:
            target = lax.rem(me_z + o, nz)
            part[g, o - 1] = jnp.dot(read, wo_ref[:, columns(target)],
                                     preferred_element_type=F32).astype(BF16)
            copy = to("sub", target, part.at[g, o - 1], part_in.at[g, o - 1],
                      rs_ss.at[g, o - 1], rs_rs.at[g, o - 1])
            copy.start()
            copies.append(copy)
        own = jnp.dot(read, wo_ref[:, columns(me_z)], preferred_element_type=F32)
        return copies, own

    def reduce_and_gather(g, copies, total):
        for o, copy in zip(others, copies):
            copy.wait()
            total = total + part_in[g, o - 1].astype(F32)
        state[g, 0] = (state[g, 0].astype(F32) + total).astype(BF16)
        gathers = []
        for o in others:
            target = lax.rem(me_z + o, nz)
            copy = to("sub", target, state.at[g, 0], state.at[g, o],
                      ag_ss.at[g, o - 1], ag_rs.at[g, o - 1])
            copy.start()
            gathers.append(copy)
        return gathers

    for g in range(2):
        for o in range(nz):
            source = lax.rem(me_z + nz - o, nz)
            state[g, o] = summary_ref[pl.ds(g * half, half), columns(source)]
    late_loads[1].wait()
    projected = [sum(project_chunk(g, o) for o in range(nz)) for g in range(2)]
    late_loads[2].wait()
    for copy in fin_copies:
        copy.wait()
    scatters = [read_and_scatter(g, projected[g]) for g in range(2)]
    for step in range(STEPS):
        more = step < STEPS - 1
        gathers = []
        for g in range(2):
            work()
            gathers.append(reduce_and_gather(g, *scatters[g]))
            if more:
                projected[g] = project_chunk(g, 0)
        for g in range(2):
            work()
            for o, copy in zip(others, gathers[g]):
                copy.wait()
                if more:
                    projected[g] = projected[g] + project_chunk(g, o)
            if more:
                scatters[g] = read_and_scatter(g, projected[g])
    for g in range(2):
        for o in range(nz):
            source = lax.rem(me_z + nz - o, nz)
            sum_ref[pl.ds(g * half, half), columns(source)] = state[g, o]


def hand_on_kernel(attended, summarized, attended_out, summarized_out, sem):
    rows = attended.shape[0] // 4
    copies = [pltpu.make_async_copy(summarized, summarized_out, sem.at[4])]
    for i in range(4):
        piece = pl.ds(i * rows, rows)
        copies.append(pltpu.make_async_copy(attended.at[piece], attended_out.at[piece], sem.at[i]))
    for copy in copies:
        copy.start()
    for copy in copies:
        copy.wait()


def on_device(queries, keys, values, decay, gate, summary, wq_sum, wo_sum):
    ns, nz = lax.axis_size("seq"), lax.axis_size("sub")
    heads = gate.shape[0]
    tokens, width = queries.shape
    rows, model = summary.shape
    cols = model // nz
    slice_rows = DH // ns
    whole = pl.BlockSpec(memory_space=pltpu.VMEM)
    scalars = pl.BlockSpec(memory_space=pltpu.SMEM)
    anywhere = pl.BlockSpec(memory_space=pl.ANY)
    sems = lambda *count: pltpu.SemaphoreType.DMA(count)
    half = rows // 2
    results = pl.pallas_call(
        functools.partial(kernel, ns, nz, heads),
        out_shape=(
            pltpu.VMEM((tokens, width), BF16),
            pltpu.VMEM((rows, model), BF16),
        ),
        in_specs=[scalars, scalars, whole] + [anywhere] * 5,
        out_specs=(whole, whole),
        scratch_shapes=[
            pltpu.VMEM((tokens, width), BF16),
            pltpu.VMEM((tokens, width), BF16),
            pltpu.VMEM((tokens, width), BF16),
            pltpu.VMEM((model, width), BF16),
            pltpu.VMEM((width, model), BF16),
            pltpu.VMEM((tokens, width), F32),
            pltpu.VMEM((ns, heads, slice_rows, DH), BF16),
            pltpu.VMEM((ns, heads, slice_rows, DH), BF16),
            pltpu.VMEM((ns, heads, slice_rows, DH), BF16),
            pltpu.VMEM((ns, heads, slice_rows, DH), BF16),
            pltpu.VMEM((ns, heads, slice_rows, DH), BF16),
            pltpu.VMEM((ns, 8, width), F32),
            pltpu.VMEM((2, nz - 1, half, cols), BF16),
            pltpu.VMEM((2, nz - 1, half, cols), BF16),
            pltpu.VMEM((2, nz, half, cols), BF16),
            sems(2 * heads + 3),
            sems(heads, ns - 1), sems(heads, ns - 1), sems(heads, ns - 1), sems(heads, ns - 1),
            sems(ns - 1), sems(ns - 1), sems(ns - 1), sems(ns - 1),
            sems(2, nz - 1), sems(2, nz - 1), sems(2, nz - 1), sems(2, nz - 1),
        ],
        compiler_params=pltpu.CompilerParams(
            collective_id=0, has_side_effects=True, vmem_limit_bytes=58 * 1024 * 1024
        ),
        cost_estimate=pl.CostEstimate(
            flops=7 * 10**9, bytes_accessed=12 * 2**20, transcendentals=6 * 10**6
        ),
    )(decay.T, gate, summary, queries, keys, values, wq_sum, wo_sum)
    return pl.pallas_call(
        hand_on_kernel,
        out_shape=(
            jax.ShapeDtypeStruct((tokens, width), BF16),
            jax.ShapeDtypeStruct((rows, model), BF16),
        ),
        in_specs=[whole] * 2,
        out_specs=(anywhere, anywhere),
        scratch_shapes=[sems(5)],
        compiler_params=pltpu.CompilerParams(vmem_limit_bytes=16 * 1024 * 1024),
    )(*results)


def solution(mesh):
    placed = (
        P(("book", "seq"), "sub"),
        P(("book", "seq"), "sub"),
        P(("book", "seq"), "sub"),
        P("book", "sub"),
        P("sub"),
        P(("book", "seq"), None),
        P(None, "sub"),
        P("sub", None),
    )
    return jax.shard_map(
        on_device,
        mesh=mesh,
        in_specs=placed,
        out_specs=(P(("book", "seq"), "sub"), P(("book", "seq"), None)),
        check_vma=False,
    )
```

```python
import functools

import jax
import jax.numpy as jnp
from jax import lax
from jax.experimental import pallas as pl
from jax.experimental.pallas import tpu as pltpu
from jax.sharding import PartitionSpec as P

STEPS = 4
DH = 256
BLOCK = 256
LOG2E = 1.4426950408889634
F32 = jnp.float32
BF16 = jnp.bfloat16


def phi(x):
    return jnp.where(x > 0, x + 1.0, jnp.exp(jnp.minimum(x, 0.0)))


def rms(x):
    return x * lax.rsqrt(jnp.mean(x * x, axis=-1, keepdims=True) + 1e-06)


def kernel(
    ns, nz, heads,
    decay_ref, gate_ref, summary_ref, q_hbm, k_hbm, v_hbm, wq_hbm, wo_hbm,
    out_ref, sum_ref,
    q_ref, k_ref, v_ref, wq_ref, wo_ref,
    local_ref, mem_out, mem_in, prior_out, prior, final, nrm,
    part, part_in, state,
    load_sem, mem_ss, mem_rs, fin_ss, fin_rs, pri_ss, pri_rs, nrm_ss, nrm_rs,
    rs_ss, rs_rs, ag_ss, ag_rs,
):
    tokens = q_ref.shape[0]
    width = heads * DH
    slice_rows = DH // ns
    cols = wo_ref.shape[1] // nz
    blocks = tokens // BLOCK
    me_s = lax.axis_index("seq")
    me_z = lax.axis_index("sub")

    def load(i, src, dst):
        return pltpu.make_async_copy(src, dst, load_sem.at[i])

    early_loads = []
    for h in range(heads):
        col = pl.ds(h * DH, DH)
        early_loads.append((load(2 * h, k_hbm.at[:, col], k_ref.at[:, col]),
                            load(2 * h + 1, v_hbm.at[:, col], v_ref.at[:, col])))
    for pair in early_loads:
        for one in pair:
            one.start()
    late_loads = [load(2 * heads, q_hbm, q_ref), load(2 * heads + 1, wq_hbm, wq_ref),
                  load(2 * heads + 2, wo_hbm, wo_ref)]

    barrier = pltpu.get_barrier_semaphore()
    for o in range(1, ns):
        pl.semaphore_signal(barrier, inc=1, device_id={"seq": lax.rem(me_s + o, ns)},
                            device_id_type=pl.DeviceIdType.MESH)
    for o in range(1, nz):
        pl.semaphore_signal(barrier, inc=1, device_id={"sub": lax.rem(me_z + o, nz)},
                            device_id_type=pl.DeviceIdType.MESH)
    pl.semaphore_wait(barrier, ns - 1 + nz - 1)

    def to(axis, target, src, dst, ss, rs):
        return pltpu.make_async_remote_copy(
            src_ref=src, dst_ref=dst, send_sem=ss, recv_sem=rs,
            device_id={axis: target}, device_id_type=pl.DeviceIdType.MESH)

    mem_copies = [[] for _ in range(heads)]
    for h in range(heads):
        for one in early_loads[h]:
            one.wait()
        if h == heads - 1:
            for one in late_loads:
                one.start()
        col = pl.ds(h * DH, DH)
        lifted = phi(k_ref[:, col].astype(F32))
        update = lax.dot_general(lifted.astype(BF16), v_ref[:, col], (((0,), (0,)), ((), ())),
                                 preferred_element_type=F32).astype(BF16)
        mem_out[:, h] = update.reshape(ns, slice_rows, DH)
        for o in range(1, ns):
            target = lax.rem(me_s + o, ns)
            copy = to("seq", target, mem_out.at[target, h], mem_in.at[me_s, h],
                      mem_ss.at[h, o - 1], mem_rs.at[h, o - 1])
            copy.start()
            mem_copies[h].append(copy)
        nrm[me_s, :, col] = jnp.broadcast_to(jnp.sum(lifted, axis=0, keepdims=True), (8, DH))
    nrm_copies = []
    for o in range(1, ns):
        target = lax.rem(me_s + o, ns)
        copy = to("seq", target, nrm.at[me_s], nrm.at[me_s], nrm_ss.at[o - 1], nrm_rs.at[o - 1])
        copy.start()
        nrm_copies.append(copy)
    mem_in[me_s] = mem_out[me_s]

    scale = DH ** (-0.5) * LOG2E

    def attend(block, h):
        rows = pl.ds(block * BLOCK, BLOCK)
        col = pl.ds(h * DH, DH)
        span = (block + 1) * BLOCK
        scores = lax.dot_general(q_ref[rows, col], k_ref[pl.ds(0, span), col],
                                 (((1,), (1,)), ((), ())), preferred_element_type=F32)
        at_row = lax.broadcasted_iota(jnp.int32, (BLOCK, BLOCK), 0)
        at_col = lax.broadcasted_iota(jnp.int32, (BLOCK, BLOCK), 1)
        last = jnp.where(at_col <= at_row, scores[:, span - BLOCK:], -jnp.inf)
        if block:
            scores = jnp.concatenate([scores[:, : span - BLOCK], last], axis=1)
        else:
            scores = last
        top = jnp.max(scores, axis=1, keepdims=True)
        weights = jnp.exp2((scores - top) * scale)
        total = jnp.sum(weights, axis=1, keepdims=True)
        mixed = jnp.dot(weights.astype(BF16), v_ref[pl.ds(0, span), col],
                        preferred_element_type=F32)
        local_ref[rows, col] = mixed / total

    def finish(block, h, prior_norm):
        rows = pl.ds(block * BLOCK, BLOCK)
        col = pl.ds(h * DH, DH)
        lifted = phi(q_ref[rows, col].astype(F32))
        below = jnp.sum(lifted * prior_norm[:, h * DH:(h + 1) * DH], axis=1, keepdims=True) + 1.0
        above = jnp.dot(lifted.astype(BF16), prior[:, h].reshape(DH, DH),
                        preferred_element_type=F32)
        blend = 1.0 / (1.0 + jnp.exp(-jnp.full((1, DH), gate_ref[h], F32)))
        mixed = blend * (above / below) + (1.0 - blend) * local_ref[rows, col]
        out_ref[rows, col] = rms(mixed).astype(BF16)

    order = []
    for h in range(heads):
        for i in range((blocks + 1) // 2):
            order += [(b, h) for b in sorted({blocks - 1 - i, i}, reverse=True)]
    weights = [8, 8] + [1, 3, 3, 1, 1, 1] * (STEPS - 1) + [1, 3, 3, 3, 2, 2]
    first_finish = 4
    total_cost = sum(block + 2 for block, _ in order)
    plan = []
    spent, deferred = 0, []
    for phase in range(len(weights)):
        aim = total_cost * sum(weights[: phase + 1]) / sum(weights)
        now = []
        while (order or (deferred and phase >= first_finish)) and (
            spent < aim or phase == len(weights) - 1
        ):
            if order:
                block, h = order.pop(0)
                now.append(("attend", block, h))
                spent += block + 1
                if phase >= first_finish:
                    now.append(("finish", block, h))
                    spent += 1
                else:
                    deferred.append((block, h))
            else:
                block, h = deferred.pop(0)
                now.append(("finish", block, h))
                spent += 1
        plan.append(now)
    plan = iter(plan)
    ready = {}

    def work():
        for what, block, h in next(plan):
            if what == "attend":
                attend(block, h)
            else:
                if "prior" not in ready:
                    for copy in pri_copies:
                        copy.wait()
                    ready["prior"] = True
                finish(block, h, ready["prior_norm"])

    late_loads[0].wait()
    work()

    fin_copies, pri_copies = [], []
    for h in range(heads):
        for copy in mem_copies[h]:
            copy.wait()
        running = jnp.zeros((slice_rows, DH), F32)
        for s in range(ns):
            prior_out[s, h] = running.astype(BF16)
            running = decay_ref[h, s] * running + mem_in[s, h].astype(F32)
        final[me_s, h] = running.astype(BF16)
        for o in range(1, ns):
            target = lax.rem(me_s + o, ns)
            copy = to("seq", target, final.at[me_s, h], final.at[me_s, h],
                      fin_ss.at[h, o - 1], fin_rs.at[h, o - 1])
            copy.start()
            fin_copies.append(copy)
    for o in range(1, ns):
        target = lax.rem(me_s + o, ns)
        copy = to("seq", target, prior_out.at[target], prior.at[me_s],
                  pri_ss.at[o - 1], pri_rs.at[o - 1])
        copy.start()
        pri_copies.append(copy)
    prior[me_s] = prior_out[me_s]

    work()

    for copy in nrm_copies:
        copy.wait()
    prior_parts, final_parts = [], []
    for h in range(heads):
        running = jnp.zeros((1, DH), F32)
        before = running
        for s in range(ns):
            before = jnp.where(me_s == s, running, before)
            running = decay_ref[h, s] * running + nrm[s, 0:1, h * DH:(h + 1) * DH]
        prior_parts.append(before)
        final_parts.append(running)
    ready["prior_norm"] = jnp.concatenate(prior_parts, axis=1)

    half = sum_ref.shape[0] // 2

    def columns(index):
        return pl.ds(pl.multiple_of(index * cols, cols), cols)

    def partner(o):
        there, bit = me_z, 1
        while bit < nz:
            if o & bit:
                there = there + bit - 2 * bit * lax.rem(lax.div(me_z, bit), 2)
            bit *= 2
        return there

    others = sorted(range(1, nz), key=lambda o: o % 2)
    across = list(range(2, nz, 2))

    def project_chunk(g, o):
        source = partner(o)
        return jnp.dot(state[g, o], wq_ref[columns(source), :], preferred_element_type=F32)

    def read_and_scatter(g, projected):
        lifted = phi(projected)
        reads = []
        for h in range(heads):
            mine = lifted[:, h * DH:(h + 1) * DH]
            below = jnp.sum(mine * final_parts[h], axis=1, keepdims=True) + 1.0
            above = jnp.dot(mine.astype(BF16), final[:, h].reshape(DH, DH),
                            preferred_element_type=F32)
            reads.append(rms(above / below).astype(BF16))
        read = jnp.concatenate(reads, axis=1) if heads > 1 else reads[0]
        copies = []
        for o in others:
            target = partner(o)
            part[g, o - 1] = jnp.dot(read, wo_ref[:, columns(target)],
                                     preferred_element_type=F32).astype(BF16)
            copy = to("sub", target, part.at[g, o - 1], part_in.at[g, o - 1],
                      rs_ss.at[g, o - 1], rs_rs.at[g, o - 1])
            copy.start()
            copies.append(copy)
        own = jnp.dot(read, wo_ref[:, columns(me_z)], preferred_element_type=F32)
        return copies, own

    def reduce_and_gather(g, copies, total):
        for o, copy in zip(others, copies):
            copy.wait()
            total = total + part_in[g, o - 1].astype(F32)
        state[g, 0] = (state[g, 0].astype(F32) + total).astype(BF16)
        return {o: gather(g, o, 0, partner(o)) for o in across + [1]}

    def gather(g, o, held, target):
        copy = to("sub", target, state.at[g, held], state.at[g, o],
                  ag_ss.at[g, o - 1], ag_rs.at[g, o - 1])
        copy.start()
        return copy

    for g in range(2):
        for o in range(nz):
            source = partner(o)
            state[g, o] = summary_ref[pl.ds(g * half, half), columns(source)]
    late_loads[1].wait()
    projected = [sum(project_chunk(g, o) for o in range(nz)) for g in range(2)]
    late_loads[2].wait()
    for copy in fin_copies:
        copy.wait()
    scatters = [read_and_scatter(g, projected[g]) for g in range(2)]
    for step in range(STEPS):
        more = step < STEPS - 1
        gathers, forwards = [], []
        for g in range(2):
            work()
            gathers.append(reduce_and_gather(g, *scatters[g]))
            if more:
                projected[g] = project_chunk(g, 0)
        for g in range(2):
            work()
            sent = {}
            for o in across:
                gathers[g][o].wait()
                sent[o + 1] = gather(g, o + 1, o, partner(1))
            forwards.append(sent)
            gathers[g][1].wait()
            if more:
                for o in across + [1]:
                    projected[g] = projected[g] + project_chunk(g, o)
        for g in range(2):
            work()
            for o, copy in forwards[g].items():
                copy.wait()
                if more:
                    projected[g] = projected[g] + project_chunk(g, o)
            if more:
                scatters[g] = read_and_scatter(g, projected[g])
    for g in range(2):
        for o in range(nz):
            source = partner(o)
            sum_ref[pl.ds(g * half, half), columns(source)] = state[g, o]


def hand_on_kernel(attended, summarized, attended_out, summarized_out, sem):
    rows = attended.shape[0] // 4
    copies = [pltpu.make_async_copy(summarized, summarized_out, sem.at[4])]
    for i in range(4):
        piece = pl.ds(i * rows, rows)
        copies.append(pltpu.make_async_copy(attended.at[piece], attended_out.at[piece], sem.at[i]))
    for copy in copies:
        copy.start()
    for copy in copies:
        copy.wait()


def on_device(queries, keys, values, decay, gate, summary, wq_sum, wo_sum):
    ns, nz = lax.axis_size("seq"), lax.axis_size("sub")
    heads = gate.shape[0]
    tokens, width = queries.shape
    rows, model = summary.shape
    cols = model // nz
    slice_rows = DH // ns
    whole = pl.BlockSpec(memory_space=pltpu.VMEM)
    scalars = pl.BlockSpec(memory_space=pltpu.SMEM)
    anywhere = pl.BlockSpec(memory_space=pl.ANY)
    sems = lambda *count: pltpu.SemaphoreType.DMA(count)
    half = rows // 2
    results = pl.pallas_call(
        functools.partial(kernel, ns, nz, heads),
        out_shape=(
            pltpu.VMEM((tokens, width), BF16),
            pltpu.VMEM((rows, model), BF16),
        ),
        in_specs=[scalars, scalars, whole] + [anywhere] * 5,
        out_specs=(whole, whole),
        scratch_shapes=[
            pltpu.VMEM((tokens, width), BF16),
            pltpu.VMEM((tokens, width), BF16),
            pltpu.VMEM((tokens, width), BF16),
            pltpu.VMEM((model, width), BF16),
            pltpu.VMEM((width, model), BF16),
            pltpu.VMEM((tokens, width), F32),
            pltpu.VMEM((ns, heads, slice_rows, DH), BF16),
            pltpu.VMEM((ns, heads, slice_rows, DH), BF16),
            pltpu.VMEM((ns, heads, slice_rows, DH), BF16),
            pltpu.VMEM((ns, heads, slice_rows, DH), BF16),
            pltpu.VMEM((ns, heads, slice_rows, DH), BF16),
            pltpu.VMEM((ns, 8, width), F32),
            pltpu.VMEM((2, nz - 1, half, cols), BF16),
            pltpu.VMEM((2, nz - 1, half, cols), BF16),
            pltpu.VMEM((2, nz, half, cols), BF16),
            sems(2 * heads + 3),
            sems(heads, ns - 1), sems(heads, ns - 1), sems(heads, ns - 1), sems(heads, ns - 1),
            sems(ns - 1), sems(ns - 1), sems(ns - 1), sems(ns - 1),
            sems(2, nz - 1), sems(2, nz - 1), sems(2, nz - 1), sems(2, nz - 1),
        ],
        compiler_params=pltpu.CompilerParams(
            collective_id=0, has_side_effects=True, vmem_limit_bytes=58 * 1024 * 1024
        ),
        cost_estimate=pl.CostEstimate(
            flops=7 * 10**9, bytes_accessed=12 * 2**20, transcendentals=6 * 10**6
        ),
    )(decay.T, gate, summary, queries, keys, values, wq_sum, wo_sum)
    return pl.pallas_call(
        hand_on_kernel,
        out_shape=(
            jax.ShapeDtypeStruct((tokens, width), BF16),
            jax.ShapeDtypeStruct((rows, model), BF16),
        ),
        in_specs=[whole] * 2,
        out_specs=(anywhere, anywhere),
        scratch_shapes=[sems(5)],
        compiler_params=pltpu.CompilerParams(vmem_limit_bytes=16 * 1024 * 1024),
    )(*results)


def solution(mesh):
    placed = (
        P(("book", "seq"), "sub"),
        P(("book", "seq"), "sub"),
        P(("book", "seq"), "sub"),
        P("book", "sub"),
        P("sub"),
        P(("book", "seq"), None),
        P(None, "sub"),
        P("sub", None),
    )
    return jax.shard_map(
        on_device,
        mesh=mesh,
        in_specs=placed,
        out_specs=(P(("book", "seq"), "sub"), P(("book", "seq"), None)),
        check_vma=False,
    )
```

```python
import functools

import jax
import jax.numpy as jnp
from jax import lax
from jax.experimental import pallas as pl
from jax.experimental.pallas import tpu as pltpu
from jax.sharding import PartitionSpec as P

STEPS = 4
DH = 256
BLOCK = 256
LOG2E = 1.4426950408889634
F32 = jnp.float32
BF16 = jnp.bfloat16


def phi(x):
    return jnp.where(x > 0, x + 1.0, jnp.exp(x))


def rms(x):
    return x * lax.rsqrt(jnp.mean(x * x, axis=-1, keepdims=True) + 1e-06)


def kernel(
    ns, nz, heads,
    decay_ref, gate_ref, summary_ref, q_hbm, k_hbm, v_hbm, wq_hbm, wo_hbm,
    out_ref, sum_ref,
    q_ref, k_ref, v_ref, wq_ref, wo_ref,
    local_ref, mem_out, mem_in, prior_out, prior, final, nrm,
    part, part_in, state,
    load_sem, mem_ss, mem_rs, fin_ss, fin_rs, pri_ss, pri_rs, nrm_ss, nrm_rs,
    rs_ss, rs_rs, ag_ss, ag_rs,
):
    tokens = q_ref.shape[0]
    width = heads * DH
    slice_rows = DH // ns
    cols = wo_ref.shape[1] // nz
    blocks = tokens // BLOCK
    me_s = lax.axis_index("seq")
    me_z = lax.axis_index("sub")

    def load(i, src, dst):
        return pltpu.make_async_copy(src, dst, load_sem.at[i])

    early_loads = []
    for h in range(heads):
        col = pl.ds(h * DH, DH)
        early_loads.append((load(2 * h, k_hbm.at[:, col], k_ref.at[:, col]),
                            load(2 * h + 1, v_hbm.at[:, col], v_ref.at[:, col])))
    for pair in early_loads:
        for one in pair:
            one.start()
    late_loads = [load(2 * heads, q_hbm, q_ref), load(2 * heads + 1, wq_hbm, wq_ref),
                  load(2 * heads + 2, wo_hbm, wo_ref)]

    barrier = pltpu.get_barrier_semaphore()
    for o in range(1, ns):
        pl.semaphore_signal(barrier, inc=1, device_id={"seq": lax.rem(me_s + o, ns)},
                            device_id_type=pl.DeviceIdType.MESH)
    for o in range(1, nz):
        pl.semaphore_signal(barrier, inc=1, device_id={"sub": lax.rem(me_z + o, nz)},
                            device_id_type=pl.DeviceIdType.MESH)
    pl.semaphore_wait(barrier, ns - 1 + nz - 1)

    def to(axis, target, src, dst, ss, rs):
        return pltpu.make_async_remote_copy(
            src_ref=src, dst_ref=dst, send_sem=ss, recv_sem=rs,
            device_id={axis: target}, device_id_type=pl.DeviceIdType.MESH)

    mem_copies = [[] for _ in range(heads)]
    for h in range(heads):
        for one in early_loads[h]:
            one.wait()
        if h == heads - 1:
            for one in late_loads:
                one.start()
        col = pl.ds(h * DH, DH)
        lifted = phi(k_ref[:, col].astype(F32))
        update = lax.dot_general(lifted.astype(BF16), v_ref[:, col], (((0,), (0,)), ((), ())),
                                 preferred_element_type=F32).astype(BF16)
        mem_out[:, h] = update.reshape(ns, slice_rows, DH)
        for o in range(1, ns):
            target = lax.rem(me_s + o, ns)
            copy = to("seq", target, mem_out.at[target, h], mem_in.at[me_s, h],
                      mem_ss.at[h, o - 1], mem_rs.at[h, o - 1])
            copy.start()
            mem_copies[h].append(copy)
        nrm[me_s, :, col] = jnp.broadcast_to(jnp.sum(lifted, axis=0, keepdims=True), (8, DH))
    nrm_copies = []
    for o in range(1, ns):
        target = lax.rem(me_s + o, ns)
        copy = to("seq", target, nrm.at[me_s], nrm.at[me_s], nrm_ss.at[o - 1], nrm_rs.at[o - 1])
        copy.start()
        nrm_copies.append(copy)
    mem_in[me_s] = mem_out[me_s]

    scale = DH ** (-0.5) * LOG2E

    def attend(block, h):
        rows = pl.ds(block * BLOCK, BLOCK)
        col = pl.ds(h * DH, DH)
        span = (block + 1) * BLOCK
        at_row = lax.broadcasted_iota(jnp.int32, (BLOCK, BLOCK), 0)
        at_col = lax.broadcasted_iota(jnp.int32, (BLOCK, BLOCK), 1)
        starts = list(range(0, span - BLOCK, 2 * BLOCK)) + [span - BLOCK, span]
        keys = [pl.ds(a, b - a) for a, b in zip(starts[:-1], starts[1:])]
        scores = [lax.dot_general(q_ref[rows, col], k_ref[part_keys, col],
                                  (((1,), (1,)), ((), ())), preferred_element_type=F32)
                  for part_keys in keys]
        scores[-1] = jnp.where(at_col <= at_row, scores[-1], -jnp.inf)
        top = functools.reduce(
            jnp.maximum, [jnp.max(piece, axis=1, keepdims=True) for piece in scores])
        total, mixed = 0.0, 0.0
        for part_keys, piece in zip(keys, scores):
            weights = jnp.exp2((piece - top) * scale)
            total = total + jnp.sum(weights, axis=1, keepdims=True)
            mixed = mixed + jnp.dot(weights.astype(BF16), v_ref[part_keys, col],
                                    preferred_element_type=F32)
        local_ref[rows, col] = mixed * (1.0 / total)

    def finish(block, h, prior_norm):
        rows = pl.ds(block * BLOCK, BLOCK)
        col = pl.ds(h * DH, DH)
        lifted = phi(q_ref[rows, col].astype(F32))
        below = jnp.sum(lifted * prior_norm[:, h * DH:(h + 1) * DH], axis=1, keepdims=True) + 1.0
        above = jnp.dot(lifted.astype(BF16), prior[:, h].reshape(DH, DH),
                        preferred_element_type=F32)
        blend = 1.0 / (1.0 + jnp.exp(-jnp.full((1, DH), gate_ref[h], F32)))
        mixed = (blend * (1.0 / below)) * above + (1.0 - blend) * local_ref[rows, col]
        out_ref[rows, col] = rms(mixed).astype(BF16)

    order = []
    for h in range(heads):
        for i in range((blocks + 1) // 2):
            order += [(b, h) for b in sorted({blocks - 1 - i, i}, reverse=True)]
    weights = [8, 8] + [1, 4, 4, 1] * (STEPS - 1) + [1, 4, 4, 4]
    first_finish = 4
    total_cost = sum(block + 2 for block, _ in order)
    plan = []
    spent, deferred = 0, []
    for phase in range(len(weights)):
        aim = total_cost * sum(weights[: phase + 1]) / sum(weights)
        now = []
        while (order or (deferred and phase >= first_finish)) and (
            spent < aim or phase == len(weights) - 1
        ):
            if order:
                block, h = order.pop(0)
                now.append(("attend", block, h))
                spent += block + 1
                if phase >= first_finish:
                    now.append(("finish", block, h))
                    spent += 1
                else:
                    deferred.append((block, h))
            else:
                block, h = deferred.pop(0)
                now.append(("finish", block, h))
                spent += 1
        plan.append(now)
    plan = iter(plan)
    ready = {}

    def work():
        for what, block, h in next(plan):
            if what == "attend":
                attend(block, h)
            else:
                if "prior" not in ready:
                    for copy in pri_copies:
                        copy.wait()
                    ready["prior"] = True
                finish(block, h, ready["prior_norm"])

    late_loads[0].wait()
    work()

    fin_copies, pri_copies = [], []
    for h in range(heads):
        for copy in mem_copies[h]:
            copy.wait()
        running = jnp.zeros((slice_rows, DH), F32)
        for s in range(ns):
            prior_out[s, h] = running.astype(BF16)
            running = decay_ref[h, s] * running + mem_in[s, h].astype(F32)
        final[me_s, h] = running.astype(BF16)
        for o in range(1, ns):
            target = lax.rem(me_s + o, ns)
            copy = to("seq", target, final.at[me_s, h], final.at[me_s, h],
                      fin_ss.at[h, o - 1], fin_rs.at[h, o - 1])
            copy.start()
            fin_copies.append(copy)
    for o in range(1, ns):
        target = lax.rem(me_s + o, ns)
        copy = to("seq", target, prior_out.at[target], prior.at[me_s],
                  pri_ss.at[o - 1], pri_rs.at[o - 1])
        copy.start()
        pri_copies.append(copy)
    prior[me_s] = prior_out[me_s]

    work()

    for copy in nrm_copies:
        copy.wait()
    prior_parts, final_parts = [], []
    for h in range(heads):
        running = jnp.zeros((1, DH), F32)
        before = running
        for s in range(ns):
            before = jnp.where(me_s == s, running, before)
            running = decay_ref[h, s] * running + nrm[s, 0:1, h * DH:(h + 1) * DH]
        prior_parts.append(before)
        final_parts.append(running)
    ready["prior_norm"] = jnp.concatenate(prior_parts, axis=1)

    half = sum_ref.shape[0] // 2

    def columns(index):
        return pl.ds(pl.multiple_of(index * cols, cols), cols)

    others = sorted(range(1, nz), key=lambda o: abs(2 * o - nz))

    def project_chunk(g, o):
        source = lax.rem(me_z + nz - o, nz)
        return jnp.dot(state[g, o], wq_ref[columns(source), :], preferred_element_type=F32)

    def read_and_scatter(g, projected):
        lifted = phi(projected)
        reads = []
        for h in range(heads):
            mine = lifted[:, h * DH:(h + 1) * DH]
            below = jnp.sum(mine * final_parts[h], axis=1, keepdims=True) + 1.0
            above = jnp.dot(mine.astype(BF16), final[:, h].reshape(DH, DH),
                            preferred_element_type=F32)
            reads.append(rms(above * (1.0 / below)).astype(BF16))
        read = jnp.concatenate(reads, axis=1) if heads > 1 else reads[0]
        copies = []
        for o in others:
            target = lax.rem(me_z + o, nz)
            part[g, o - 1] = jnp.dot(read, wo_ref[:, columns(target)],
                                     preferred_element_type=F32).astype(BF16)
            copy = to("sub", target, part.at[g, o - 1], part_in.at[g, o - 1],
                      rs_ss.at[g, o - 1], rs_rs.at[g, o - 1])
            copy.start()
            copies.append(copy)
        own = jnp.dot(read, wo_ref[:, columns(me_z)], preferred_element_type=F32)
        return copies, own

    def reduce_and_gather(g, copies, total):
        for o, copy in zip(others, copies):
            copy.wait()
            total = total + part_in[g, o - 1].astype(F32)
        state[g, 0] = (state[g, 0].astype(F32) + total).astype(BF16)
        gathers = []
        for o in others:
            target = lax.rem(me_z + o, nz)
            copy = to("sub", target, state.at[g, 0], state.at[g, o],
                      ag_ss.at[g, o - 1], ag_rs.at[g, o - 1])
            copy.start()
            gathers.append(copy)
        return gathers

    for g in range(2):
        for o in range(nz):
            source = lax.rem(me_z + nz - o, nz)
            state[g, o] = summary_ref[pl.ds(g * half, half), columns(source)]
    late_loads[1].wait()
    projected = [sum(project_chunk(g, o) for o in range(nz)) for g in range(2)]
    late_loads[2].wait()
    for copy in fin_copies:
        copy.wait()
    scatters = [read_and_scatter(g, projected[g]) for g in range(2)]
    for step in range(STEPS):
        more = step < STEPS - 1
        gathers = []
        for g in range(2):
            work()
            gathers.append(reduce_and_gather(g, *scatters[g]))
            if more:
                projected[g] = project_chunk(g, 0)
        for g in range(2):
            work()
            for o, copy in zip(others, gathers[g]):
                copy.wait()
                if more:
                    projected[g] = projected[g] + project_chunk(g, o)
            if more:
                scatters[g] = read_and_scatter(g, projected[g])
    for g in range(2):
        for o in range(nz):
            source = lax.rem(me_z + nz - o, nz)
            sum_ref[pl.ds(g * half, half), columns(source)] = state[g, o]


def hand_on_kernel(attended, summarized, attended_out, summarized_out, sem):
    rows = attended.shape[0] // 4
    copies = [pltpu.make_async_copy(summarized, summarized_out, sem.at[4])]
    for i in range(4):
        piece = pl.ds(i * rows, rows)
        copies.append(pltpu.make_async_copy(attended.at[piece], attended_out.at[piece], sem.at[i]))
    for copy in copies:
        copy.start()
    for copy in copies:
        copy.wait()


def on_device(queries, keys, values, decay, gate, summary, wq_sum, wo_sum):
    ns, nz = lax.axis_size("seq"), lax.axis_size("sub")
    heads = gate.shape[0]
    tokens, width = queries.shape
    rows, model = summary.shape
    cols = model // nz
    slice_rows = DH // ns
    whole = pl.BlockSpec(memory_space=pltpu.VMEM)
    scalars = pl.BlockSpec(memory_space=pltpu.SMEM)
    anywhere = pl.BlockSpec(memory_space=pl.ANY)
    sems = lambda *count: pltpu.SemaphoreType.DMA(count)
    half = rows // 2
    results = pl.pallas_call(
        functools.partial(kernel, ns, nz, heads),
        out_shape=(
            pltpu.VMEM((tokens, width), BF16),
            pltpu.VMEM((rows, model), BF16),
        ),
        in_specs=[scalars, scalars, whole] + [anywhere] * 5,
        out_specs=(whole, whole),
        scratch_shapes=[
            pltpu.VMEM((tokens, width), BF16),
            pltpu.VMEM((tokens, width), BF16),
            pltpu.VMEM((tokens, width), BF16),
            pltpu.VMEM((model, width), BF16),
            pltpu.VMEM((width, model), BF16),
            pltpu.VMEM((tokens, width), F32),
            pltpu.VMEM((ns, heads, slice_rows, DH), BF16),
            pltpu.VMEM((ns, heads, slice_rows, DH), BF16),
            pltpu.VMEM((ns, heads, slice_rows, DH), BF16),
            pltpu.VMEM((ns, heads, slice_rows, DH), BF16),
            pltpu.VMEM((ns, heads, slice_rows, DH), BF16),
            pltpu.VMEM((ns, 8, width), F32),
            pltpu.VMEM((2, nz - 1, half, cols), BF16),
            pltpu.VMEM((2, nz - 1, half, cols), BF16),
            pltpu.VMEM((2, nz, half, cols), BF16),
            sems(2 * heads + 3),
            sems(heads, ns - 1), sems(heads, ns - 1), sems(heads, ns - 1), sems(heads, ns - 1),
            sems(ns - 1), sems(ns - 1), sems(ns - 1), sems(ns - 1),
            sems(2, nz - 1), sems(2, nz - 1), sems(2, nz - 1), sems(2, nz - 1),
        ],
        compiler_params=pltpu.CompilerParams(
            collective_id=0, has_side_effects=True, vmem_limit_bytes=58 * 1024 * 1024
        ),
        cost_estimate=pl.CostEstimate(
            flops=7 * 10**9, bytes_accessed=12 * 2**20, transcendentals=6 * 10**6
        ),
    )(decay.T, gate, summary, queries, keys, values, wq_sum, wo_sum)
    return pl.pallas_call(
        hand_on_kernel,
        out_shape=(
            jax.ShapeDtypeStruct((tokens, width), BF16),
            jax.ShapeDtypeStruct((rows, model), BF16),
        ),
        in_specs=[whole] * 2,
        out_specs=(anywhere, anywhere),
        scratch_shapes=[sems(5)],
        compiler_params=pltpu.CompilerParams(vmem_limit_bytes=16 * 1024 * 1024),
    )(*results)


def solution(mesh):
    placed = (
        P(("book", "seq"), "sub"),
        P(("book", "seq"), "sub"),
        P(("book", "seq"), "sub"),
        P("book", "sub"),
        P("sub"),
        P(("book", "seq"), None),
        P(None, "sub"),
        P("sub", None),
    )
    return jax.shard_map(
        on_device,
        mesh=mesh,
        in_specs=placed,
        out_specs=(P(("book", "seq"), "sub"), P(("book", "seq"), None)),
        check_vma=False,
    )
```
